256 devices in a mesh: dp: 64 (over y, x_lo, z), pair: 4 (over x_hi, core).
Axes of the slice: x: 4 (x_hi: 2, x_lo: 2; x = x_hi * 2 + x_lo), y: 4, z: 8, core: 2. Of those that a mesh axis runs over, the one named last changes fastest.
Arguments:
- student_image: bfloat16 [65536, 512], P(('dp', 'pair')), may hold values from -60 to 60
- student_text: bfloat16 [65536, 512], P(('dp', 'pair')), may hold values from -6 to 6
- teacher_image: bfloat16 [65536, 1280], P(('dp', 'pair')), may hold values from -60 to 60
- teacher_text: bfloat16 [65536, 1280], P(('dp', 'pair')), may hold values from -6 to 6
Outputs:
- grad_image: float32 [65536, 512], P(('dp', 'pair'))
- grad_text: float32 [65536, 512], P(('dp', 'pair'))
The draws below stay inside these ranges and needn't reach their ends.
All inputs are finite; a program needn't handle non-finite values.
Results may differ from the reference program's by a relative error of at most 0.0025.
Values may be sent and summed in bfloat16 or wider, within the bound.
A program may use at most 128 MiB of HBM per device.

```python
import math
import jax
import jax.numpy as jnp
from jax import lax

DS = 512
DT = 1280
WINDOW = 4
BLK = 1024
BATCH = 65536


def text_draw(key, salt, width):
    inner = jax.random.fold_in(key, salt)
    return jnp.clip(jax.random.normal(inner, (BATCH, width), jnp.float32), -6.0, 6.0)


def image_draw(key, salt, width):
    inner = jax.random.fold_in(key, salt)
    values = jax.random.normal(inner, (BATCH, width), jnp.float32)
    return jnp.clip(values, -60.0, 60.0)


def draw_student_text(key, part):
    return text_draw(key, 11, DS).astype(jnp.bfloat16)


def draw_teacher_text(key, part):
    return text_draw(key, 12, DT).astype(jnp.bfloat16)


def draw_student_image(key, part):
    return image_draw(key, 13, DS).astype(jnp.bfloat16)


def draw_teacher_image(key, part):
    return image_draw(key, 14, DT).astype(jnp.bfloat16)


def setup_inputs(seed: int = 0) -> dict:
    streams_of = jax.random.split(jax.random.key(seed), 5)
    return {
        "student_image": draw_student_image(jax.random.fold_in(streams_of[4], 71), 0),
        "student_text": draw_student_text(jax.random.fold_in(streams_of[4], 71), 0),
        "teacher_image": draw_teacher_image(jax.random.fold_in(streams_of[4], 71), 0),
        "teacher_text": draw_teacher_text(jax.random.fold_in(streams_of[4], 71), 0),
    }


def stats_of(scores, axis):
    top = lax.optimization_barrier(jnp.max(scores, axis=axis))
    total = lax.optimization_barrier(jnp.sum(jnp.exp(scores - jnp.expand_dims(top, axis)), axis=axis))
    return (top, total)

def combine_stats(first, second):
    result = []
    for offset in (0, 2):
        top = jnp.maximum(first[offset], second[offset])
        total = first[offset + 1] * jnp.exp(first[offset] - top) + second[offset + 1] * jnp.exp(second[offset] - top)
        result += [top, total]
    return tuple(result)

def reference(student_image, student_text, teacher_image, teacher_text):
    scale_s = 2.0 / math.sqrt(DS)
    scale_t = 2.0 / math.sqrt(DT)
    blocks = BATCH // BLK
    span = WINDOW * BLK
    starts = jnp.arange(blocks, dtype=jnp.int32) * BLK
    text_s = jnp.concatenate([student_text, student_text[:span]], axis=0)
    text_t = jnp.concatenate([teacher_text, teacher_text[:span]], axis=0)

    def tiles(first):
        rows_s = lax.dynamic_slice_in_dim(student_image, first, BLK, 0)
        rows_t = lax.dynamic_slice_in_dim(teacher_image, first, BLK, 0)
        win_s = lax.dynamic_slice_in_dim(text_s, first, span, 0)
        win_t = lax.dynamic_slice_in_dim(text_t, first, span, 0)
        s_tile = jnp.dot(rows_s, win_s.T, preferred_element_type=jnp.float32) * scale_s
        t_tile = jnp.dot(rows_t, win_t.T, preferred_element_type=jnp.float32) * scale_t
        return (rows_s, win_s, s_tile, t_tile)

    def first_pass(carry, first):
        rows_s, win_s, s_tile, t_tile = tiles(first)
        row_stats = stats_of(s_tile, 1) + stats_of(t_tile, 1)
        old = tuple((lax.dynamic_slice_in_dim(c, first, span, 0) for c in carry))
        new = combine_stats(old, stats_of(s_tile, 0) + stats_of(t_tile, 0))
        carry = tuple((lax.dynamic_update_slice_in_dim(c, n, first, 0) for c, n in zip(carry, new)))
        return (carry, row_stats)
    low = jnp.full((BATCH + span,), -1e+30, jnp.float32)
    nothing = jnp.zeros((BATCH + span,), jnp.float32)
    columns, rows = lax.scan(first_pass, (low, nothing, low, nothing), starts)
    head = tuple((c[:span] for c in columns))
    tail = tuple((c[BATCH:] for c in columns))
    folded = combine_stats(head, tail)
    whole = tuple((jnp.concatenate([f, c[span:BATCH]], axis=0) for f, c in zip(folded, columns)))
    extended = tuple((jnp.concatenate([c, c[:span]], axis=0) for c in whole))

    def second_pass(text_acc, packed):
        first, rm_s, rz_s, rm_t, rz_t = packed
        rows_s, win_s, s_tile, t_tile = tiles(first)
        cm_s, cz_s, cm_t, cz_t = tuple((lax.dynamic_slice_in_dim(c, first, span, 0) for c in extended))
        weights = (jnp.exp(s_tile - rm_s[:, None]) / rz_s[:, None] - jnp.exp(t_tile - rm_t[:, None]) / rz_t[:, None] + jnp.exp(s_tile - cm_s[None, :]) / cz_s[None, :] - jnp.exp(t_tile - cm_t[None, :]) / cz_t[None, :]).astype(jnp.bfloat16)
        image_part = jnp.dot(weights, win_s, preferred_element_type=jnp.float32)
        old = lax.dynamic_slice_in_dim(text_acc, first, span, 0)
        added = old + jnp.dot(weights.T, rows_s, preferred_element_type=jnp.float32)
        text_acc = lax.dynamic_update_slice_in_dim(text_acc, added, first, 0)
        return (text_acc, image_part)
    text_acc, image_parts = lax.scan(second_pass, jnp.zeros((BATCH + span, DS), jnp.float32), (starts,) + rows)
    text_sum = text_acc[:BATCH].at[:span].add(text_acc[BATCH:])
    grad_image = image_parts.reshape(BATCH, DS) * scale_s
    grad_text = text_sum * scale_s
    return (grad_image, grad_text)
```

```python
import functools
import math

import jax
import jax.numpy as jnp
from jax import lax
from jax.experimental import pallas as pl
from jax.experimental.pallas import tpu as pltpu
from jax.sharding import PartitionSpec as P

MESH = pl.DeviceIdType.MESH
F32 = jnp.float32
BF16 = jnp.bfloat16

WINDOW = 4
PAIR = 4
ROWS = 256
BLOCK = ROWS * PAIR
CHUNKS = 2
CR = ROWS // CHUNKS
TILES = WINDOW * CHUNKS
SLAB = 32
SHIFTS = (-3, -2, -1, 1, 2, 3)
NT = (((1,), (1,)), ((), ()))
NN = (((1,), (0,)), ((), ()))
TN = (((0,), (0,)), ((), ()))


def rows_of(start, size):
    return pl.ds(pl.multiple_of(start, size), size)


def kernel(
    groups, scale_s, scale_t,
    si, st, ti, tt, out_image, out_text,
    img_s, img_t, txt_s, txt_t,
    s_buf, t_buf, e_img_s, e_img_t, e_txt_s, e_txt_t, w,
    istat, ist, rist, tcol, tst, rts, tsct, tsc, asc,
    g_send, g_recv, p_own, gi, gi_sib, gi_x, gi_sum,
    local_sem, tx_send, tx_recv, im_send, im_recv,
    ts_send, ts_recv, is_send, is_recv, g_ssem, g_rsem, gi_ssem, gi_rsem,
):
    d = lax.axis_index("dp")
    p = lax.axis_index("pair")
    sib = p + 1 - 2 * lax.rem(p, 2)
    far = lax.rem(p + 2, PAIR)
    diag = 3 - p
    mates = {1: sib, 2: far, 3: diag}

    def at(shift):
        return (lax.rem(d + shift + groups, groups), p)

    def remote(src, dst, ssem, rsem, device):
        return pltpu.make_async_remote_copy(
            src_ref=src, dst_ref=dst, send_sem=ssem, recv_sem=rsem,
            device_id=device, device_id_type=MESH,
        )

    own_rows = rows_of(p * ROWS, ROWS)
    locals_ = [
        pltpu.make_async_copy(st, txt_s.at[pl.ds(0, ROWS)], local_sem.at[0]),
        pltpu.make_async_copy(tt, txt_t.at[pl.ds(0, ROWS)], local_sem.at[1]),
        pltpu.make_async_copy(si, img_s.at[own_rows], local_sem.at[2]),
        pltpu.make_async_copy(ti, img_t.at[own_rows], local_sem.at[3]),
    ]
    for copy in locals_:
        copy.start()

    barrier = pltpu.get_barrier_semaphore()
    for shift in SHIFTS:
        pl.semaphore_signal(barrier, inc=1, device_id=at(shift), device_id_type=MESH)
    for r in (1, 2, 3):
        pl.semaphore_signal(barrier, inc=1, device_id=(d, mates[r]), device_id_type=MESH)
    for copy in locals_:
        copy.wait()
    pl.semaphore_wait(barrier, 9)

    def text_copies(n):
        here, there = pl.ds(n * CR, CR), pl.ds((n + CHUNKS) * CR, CR)
        return [
            remote(buf.at[here], buf.at[there], tx_send.at[i, n], tx_recv.at[i, n], at(-1))
            for i, buf in enumerate((txt_s, txt_t))
        ]

    def send_text(n):
        for copy in text_copies(n):
            copy.start()

    def text_arrives(n):
        for copy in text_copies(n - CHUNKS):
            copy.wait_recv()

    def image_copies(slot, quarter, device):
        rows = rows_of(quarter * ROWS, ROWS)
        return [
            remote(buf.at[rows], buf.at[rows], im_send.at[i, slot], im_recv.at[i, slot], device)
            for i, buf in enumerate((img_s, img_t))
        ]

    to_far = image_copies(0, p, (d, far))
    to_sib = image_copies(1, p, (d, sib))
    pass_on = image_copies(2, far, (d, sib))
    for copy in to_far + to_sib:
        copy.start()
    for n in range(CHUNKS):
        send_text(n)
    for n in range(CHUNKS, 2 * CHUNKS):
        text_arrives(n)
        send_text(n)
    for copy in to_far:
        copy.wait_recv()
    for copy in pass_on:
        copy.start()
    for copy in to_sib + pass_on:
        copy.wait_recv()

    tcol[...] = jnp.zeros_like(tcol)
    ist[...] = jnp.zeros_like(ist)
    tsct[...] = jnp.zeros_like(tsct)

    def tile_stats(j, buf, e_img, e_txt, which):
        base = j * CR

        def by_text(g, top):
            x = buf[rows_of(g * SLAB, SLAB), :]
            m = jnp.max(x, axis=1, keepdims=True)
            e = jnp.exp(x - m)
            rows = rows_of(base + g * SLAB, SLAB)
            e_txt[rows, :] = e
            tcol[rows, which : which + 1] = m
            tcol[rows, which + 2 : which + 3] = jnp.sum(e, axis=1, keepdims=True)
            return jnp.maximum(top, jnp.max(x.reshape(SLAB // 8, 8, BLOCK), axis=0))

        top = lax.fori_loop(0, CR // SLAB, by_text, jnp.full((8, BLOCK), -jnp.inf, F32))
        top = jnp.max(top, axis=0, keepdims=True)

        def by_image(g, total):
            e = jnp.exp(buf[rows_of(g * SLAB, SLAB), :] - top)
            e_img[rows_of(base + g * SLAB, SLAB), :] = e
            return total + jnp.sum(e.reshape(SLAB // 8, 8, BLOCK), axis=0)

        total = lax.fori_loop(0, CR // SLAB, by_image, jnp.zeros((8, BLOCK), F32))
        istat[which, pl.ds(j, 1), :] = top
        istat[which + 2, pl.ds(j, 1), :] = jnp.sum(total, axis=0, keepdims=True)

    def tile(j, carry):
        for n in range(2 * CHUNKS, 3 * CHUNKS):
            @pl.when(j == 2 * (n - 2 * CHUNKS + 1))
            def _(n=n):
                text_arrives(n)
                send_text(n)
        for n in range(3 * CHUNKS, 4 * CHUNKS):
            @pl.when(j == n)
            def _(n=n):
                text_arrives(n)
        rows = rows_of(j * CR, CR)
        s_buf[...] = lax.dot_general(txt_s[rows, :], img_s[...], NT, preferred_element_type=F32) * scale_s
        t_buf[...] = lax.dot_general(txt_t[rows, :], img_t[...], NT, preferred_element_type=F32) * scale_t
        tile_stats(j, s_buf, e_img_s, e_txt_s, 0)
        tile_stats(j, t_buf, e_img_t, e_txt_t, 1)
        return carry

    lax.fori_loop(0, TILES, tile, 0)

    tst[...] = jnp.transpose(tcol[...])[0:8, :]

    def text_stat_copy(i):
        shift = SHIFTS[i]
        low, high = max(0, shift), min(WINDOW, WINDOW + shift)
        size = (high - low) * ROWS
        return remote(
            tst.at[:, pl.ds(low * ROWS, size)], rts.at[i, :, pl.ds((low - shift) * ROWS, size)],
            ts_send.at[i], ts_recv.at[i], at(shift),
        )

    for i in range(6):
        text_stat_copy(i).start()

    for which in (0, 1):
        tops, totals = istat[which], istat[which + 2]
        top = jnp.max(tops, axis=0, keepdims=True)
        ist[which : which + 1, :] = top
        ist[which + 2 : which + 3, :] = jnp.sum(totals * jnp.exp(tops - top), axis=0, keepdims=True)

    def image_stat_copy(r):
        return remote(ist, rist.at[r - 1], is_send.at[r - 1], is_recv.at[r - 1], (d, mates[r]))

    for r in (1, 2, 3):
        image_stat_copy(r).start()
    for r in (1, 2, 3):
        image_stat_copy(r).wait_recv()

    def joined(parts):
        top = functools.reduce(jnp.maximum, [a[0:2] for a in parts])
        total = functools.reduce(jnp.add, [a[2:4] * jnp.exp(a[0:2] - top) for a in parts])
        return top, total

    top, total = joined([ist[0:4, :]] + [rist[r, 0:4, :] for r in range(3)])
    for which in (0, 1):
        asc[which] = jnp.exp(istat[which] - top[which : which + 1]) / total[which : which + 1]

    for i in range(6):
        text_stat_copy(i).wait_recv()
    for k in range(WINDOW):
        cols = pl.ds(k * ROWS, ROWS)
        parts = [tst[0:4, cols]]
        for i, shift in enumerate(SHIFTS):
            if 0 <= k + shift < WINDOW:
                parts.append(rts[i, 0:4, cols])
        top, total = joined(parts)
        tsct[0:2, cols] = jnp.exp(tst[0:2, cols] - top) / total
    tsc[...] = jnp.transpose(tsct[...])

    def weights(j):
        a_s, a_t = asc[0, pl.ds(j, 1), :], asc[1, pl.ds(j, 1), :]

        def slab(g, carry):
            rows = rows_of(j * CR + g * SLAB, SLAB)
            c_s, c_t = tsc[rows, 0:1], tsc[rows, 1:2]
            w[rows, :] = (
                e_img_s[rows, :] * a_s - e_img_t[rows, :] * a_t
                + e_txt_s[rows, :] * c_s - e_txt_t[rows, :] * c_t
            ).astype(BF16)
            return carry

        lax.fori_loop(0, CR // SLAB, slab, 0)

    def text_term(j):
        weights(j)
        return lax.dot_general(
            w[rows_of(j * CR, CR), :], img_s[...], NN, preferred_element_type=F32
        ) * scale_s

    def grad_copy(hop, c):
        rows = pl.ds(c * CR, CR)
        return remote(
            g_send.at[hop, rows], g_recv.at[hop, rows], g_ssem.at[hop, c], g_rsem.at[hop, c], at(1)
        )

    for c in range(CHUNKS):
        g_send[0, pl.ds(c * CR, CR), :] = text_term(3 * CHUNKS + c)
        grad_copy(0, c).start()

    def earlier(j, carry):
        p_own[rows_of(j * CR, CR), :] = text_term(j)
        return carry

    lax.fori_loop(0, 3 * CHUNKS, earlier, 0)

    def image_term(quarter):
        return lax.dot_general(
            w[:, rows_of(quarter * ROWS, ROWS)], txt_s[...], TN, preferred_element_type=F32
        ) * scale_s

    order = (sib, diag, far, p)

    def sib_copy(i):
        return remote(gi.at[i], gi_sib.at[i], gi_ssem.at[i], gi_rsem.at[i], (d, sib))

    for i in (1, 0):
        gi[i] = image_term(order[i])
        sib_copy(i).start()
    for i in (2, 3):
        gi[i] = image_term(order[i])
    sib_copy(1).wait_recv()
    gi_sum[...] = gi[2] + gi_sib[1]
    far_copy = remote(gi_sum, gi_x, gi_ssem.at[2], gi_rsem.at[2], (d, far))
    far_copy.start()

    for hop in range(3):
        for c in range(CHUNKS):
            rows = pl.ds(c * CR, CR)
            mine = p_own[pl.ds((2 - hop) * ROWS + c * CR, CR), :]
            grad_copy(hop, c).wait_recv()
            if hop < 2:
                g_send[hop + 1, rows, :] = mine + g_recv[hop, rows, :]
                grad_copy(hop + 1, c).start()
            else:
                out_text[rows, :] = mine + g_recv[hop, rows, :]
        if hop == 1:
            sib_copy(0).wait_recv()
            far_copy.wait_recv()
            out_image[...] = gi[3] + gi_sib[0] + gi_x[...]

    for n in range(3 * CHUNKS):
        for copy in text_copies(n):
            copy.wait_send()
    for copy in to_far + to_sib + pass_on:
        copy.wait_send()
    for i in range(6):
        text_stat_copy(i).wait_send()
    for r in (1, 2, 3):
        image_stat_copy(r).wait_send()
    for hop in range(3):
        for c in range(CHUNKS):
            grad_copy(hop, c).wait_send()
    for i in (0, 1):
        sib_copy(i).wait_send()
    far_copy.wait_send()


def on_device(groups, student_image, student_text, teacher_image, teacher_text):
    ds, dt = student_image.shape[1], teacher_image.shape[1]
    dma = pltpu.SemaphoreType.DMA
    vmem = pltpu.VMEM
    return pl.pallas_call(
        functools.partial(kernel, groups, 2.0 / math.sqrt(ds), 2.0 / math.sqrt(dt)),
        out_shape=(
            jax.ShapeDtypeStruct((ROWS, ds), F32),
            jax.ShapeDtypeStruct((ROWS, ds), F32),
        ),
        in_specs=[pl.BlockSpec(memory_space=pl.ANY)] * 4,
        out_specs=(pl.BlockSpec(memory_space=pltpu.VMEM),) * 2,
        scratch_shapes=[
            vmem((BLOCK, ds), BF16), vmem((BLOCK, dt), BF16),
            vmem((BLOCK, ds), BF16), vmem((BLOCK, dt), BF16),
            vmem((CR, BLOCK), F32), vmem((CR, BLOCK), F32),
            vmem((BLOCK, BLOCK), F32), vmem((BLOCK, BLOCK), F32),
            vmem((BLOCK, BLOCK), F32), vmem((BLOCK, BLOCK), F32),
            vmem((BLOCK, BLOCK), BF16),
            vmem((4, TILES, BLOCK), F32), vmem((8, BLOCK), F32), vmem((3, 8, BLOCK), F32),
            vmem((BLOCK, 128), F32), vmem((8, BLOCK), F32), vmem((6, 8, BLOCK), F32),
            vmem((128, BLOCK), F32), vmem((BLOCK, 128), F32), vmem((2, TILES, BLOCK), F32),
            vmem((3, ROWS, ds), F32), vmem((3, ROWS, ds), F32), vmem((3 * ROWS, ds), F32),
            vmem((4, ROWS, ds), F32), vmem((2, ROWS, ds), F32),
            vmem((ROWS, ds), F32), vmem((ROWS, ds), F32),
            dma((4,)), dma((2, 3 * CHUNKS)), dma((2, 3 * CHUNKS)), dma((2, 3)), dma((2, 3)),
            dma((6,)), dma((6,)), dma((3,)), dma((3,)),
            dma((3, CHUNKS)), dma((3, CHUNKS)), dma((3,)), dma((3,)),
        ],
        compiler_params=pltpu.CompilerParams(
            collective_id=0, has_side_effects=True, vmem_limit_bytes=56 * 2**20
        ),
    )(student_image, student_text, teacher_image, teacher_text)


def solution(mesh):
    spec = P(("dp", "pair"), None)
    return jax.shard_map(
        functools.partial(on_device, mesh.shape["dp"]),
        mesh=mesh,
        in_specs=(spec,) * 4,
        out_specs=(spec, spec),
        check_vma=False,
    )
```

```python
import functools
import math

import jax
import jax.numpy as jnp
from jax import lax
from jax.experimental import pallas as pl
from jax.experimental.pallas import tpu as pltpu
from jax.sharding import PartitionSpec as P

MESH = pl.DeviceIdType.MESH
F32 = jnp.float32
BF16 = jnp.bfloat16

WINDOW = 4
PAIR = 4
ROWS = 256
BLOCK = ROWS * PAIR
CHUNKS = 2
CR = ROWS // CHUNKS
TILES = WINDOW * CHUNKS
SLAB = 32
SHIFTS = (-3, -2, -1, 1, 2, 3)
LINE = 8
PIECES = 4
NT = (((1,), (1,)), ((), ()))
NN = (((1,), (0,)), ((), ()))
TN = (((0,), (0,)), ((), ()))


SPAN, LOW = 240.0 * math.log(2.0), 120.0 * math.log(2.0)


def rows_of(start, size):
    return pl.ds(pl.multiple_of(start, size), size)


def encoded(x):
    rows, width = x.shape
    parts = jnp.abs(x).reshape(rows // 8, 8, width)
    top = jnp.max(parts, axis=0)
    top = functools.reduce(jnp.maximum, [top[:, i : i + 128] for i in range(0, width, 128)])
    top = jnp.maximum(top, 1e-36)
    ratio = jnp.concatenate([SPAN / top] * (width // 128), axis=1)
    size = jnp.exp(parts * ratio[None] - LOW).reshape(rows, width)
    return jnp.where(x < 0, -size, size).astype(BF16), top


def decoded(code, top):
    rows, width = code.shape
    y = code.astype(F32)
    size = (jnp.log(jnp.abs(y)) + LOW).reshape(rows // 8, 8, width)
    scale = jnp.concatenate([top * (1.0 / SPAN)] * (width // 128), axis=1)
    x = (size * scale[None]).reshape(rows, width)
    return jnp.where(y < 0, -x, x)


def kernel(
    groups, scale_s, scale_t,
    si, st, ti, tt, out_image, out_text,
    img_s, img_t, txt_s, txt_t,
    s_buf, t_buf, e_img_s, e_img_t, e_txt_s, e_txt_t, w,
    istat, ist, rist, tcol, tst, rts, tsct, tsc, asc,
    g_send, g_recv, g_stop, g_rtop, p_own, gi, gi_sib, x_send, x_recv, x_stop, x_rtop,
    local_sem, tx_send, tx_recv, im_send, im_recv,
    ts_send, ts_recv, is_send, is_recv, g_ssem, g_rsem, gi_ssem, gi_rsem,
):
    d = lax.axis_index("dp")
    p = lax.axis_index("pair")
    sib = p + 1 - 2 * lax.rem(p, 2)
    far = lax.rem(p + 2, PAIR)
    diag = 3 - p
    mates = {1: sib, 2: far, 3: diag}

    place = lax.rem(d, LINE)
    last = place == LINE - 1

    def at(shift, c):
        group = lax.rem(d + shift + groups, groups)
        if c % 2 == 0:
            return (group, p)
        turns = jnp.logical_or(place + shift < 0, place + shift >= LINE)
        return (group, jnp.where(turns, far, p))

    def remote(src, dst, ssem, rsem, device):
        return pltpu.make_async_remote_copy(
            src_ref=src, dst_ref=dst, send_sem=ssem, recv_sem=rsem,
            device_id=device, device_id_type=MESH,
        )

    own_rows = rows_of(p * ROWS, ROWS)
    locals_ = [
        pltpu.make_async_copy(si, img_s.at[own_rows], local_sem.at[0]),
        pltpu.make_async_copy(ti, img_t.at[own_rows], local_sem.at[1]),
    ]
    for c in range(CHUNKS):
        for i, (src, buf) in enumerate(((st, txt_s), (tt, txt_t))):
            locals_.append(pltpu.make_async_copy(
                src.at[pl.ds(c * CR, CR)], buf.at[pl.ds(c * WINDOW * CR, CR)], local_sem.at[2 + 2 * c + i]
            ))
    for copy in locals_:
        copy.start()

    barrier = pltpu.get_barrier_semaphore()
    for shift in SHIFTS:
        group = lax.rem(d + shift + groups, groups)
        for other in (p, far):
            pl.semaphore_signal(barrier, inc=1, device_id=(group, other), device_id_type=MESH)
    for r in (1, 2, 3):
        pl.semaphore_signal(barrier, inc=1, device_id=(d, mates[r]), device_id_type=MESH)
    for copy in locals_:
        copy.wait()
    pl.semaphore_wait(barrier, 15)

    def text_copies(k, c):
        here, there = pl.ds((c * WINDOW + k) * CR, CR), pl.ds((c * WINDOW + k + 1) * CR, CR)
        return [
            remote(buf.at[here], buf.at[there], tx_send.at[i, k, c], tx_recv.at[i, k, c], at(-1, c))
            for i, buf in enumerate((txt_s, txt_t))
        ]

    def send_text(k, c):
        for copy in text_copies(k, c):
            copy.start()

    def text_arrives(k, c):
        for copy in text_copies(k - 1, c):
            copy.wait_recv()

    def image_copies(slot, start, size, device):
        rows = rows_of(start, size)
        return [
            remote(buf.at[rows], buf.at[rows], im_send.at[i, slot], im_recv.at[i, slot], device)
            for i, buf in enumerate((img_s, img_t))
        ]

    size = ROWS // PIECES
    to_far = [image_copies(2 + i, p * ROWS + i * size, size, (d, far)) for i in range(PIECES)]
    to_sib = image_copies(0, p * ROWS, ROWS, (d, sib))
    pass_on = image_copies(1, far * ROWS, ROWS, (d, sib))

    def send_far(i):
        for copy in to_far[i]:
            copy.start()

    for copy in to_sib:
        copy.start()
    send_text(0, 0)
    send_far(0)
    for c in range(1, CHUNKS):
        send_text(0, c)

    @pl.when(jnp.logical_not(last))
    def _():
        for i in range(1, PIECES):
            send_far(i)

    early = [(1, c) for c in range(CHUNKS)] + [(2, c) for c in range(CHUNKS - 1)]
    for i, (k, c) in enumerate(early):
        text_arrives(k, c)
        send_text(k, c)
        if i + 1 < PIECES:
            @pl.when(last)
            def _(i=i):
                send_far(i + 1)
    for piece in to_far:
        for copy in piece:
            copy.wait_recv()
    for copy in pass_on:
        copy.start()
    for copy in to_sib + pass_on:
        copy.wait_recv()

    tcol[...] = jnp.zeros_like(tcol)
    ist[...] = jnp.zeros_like(ist)
    tsct[...] = jnp.zeros_like(tsct)

    def tile_stats(j, buf, e_img, e_txt, which):
        base = j * CR

        def by_text(g, top):
            x = buf[rows_of(g * SLAB, SLAB), :]
            m = jnp.max(x, axis=1, keepdims=True)
            e = jnp.exp(x - m)
            rows = rows_of(base + g * SLAB, SLAB)
            e_txt[rows, :] = e
            tcol[rows, which : which + 1] = m
            tcol[rows, which + 2 : which + 3] = jnp.sum(e, axis=1, keepdims=True)
            return jnp.maximum(top, jnp.max(x.reshape(SLAB // 8, 8, BLOCK), axis=0))

        top = lax.fori_loop(0, CR // SLAB, by_text, jnp.full((8, BLOCK), -jnp.inf, F32))
        top = jnp.max(top, axis=0, keepdims=True)

        def by_image(g, total):
            e = jnp.exp(buf[rows_of(g * SLAB, SLAB), :] - top)
            e_img[rows_of(base + g * SLAB, SLAB), :] = e
            return total + jnp.sum(e.reshape(SLAB // 8, 8, BLOCK), axis=0)

        total = lax.fori_loop(0, CR // SLAB, by_image, jnp.zeros((8, BLOCK), F32))
        istat[which, pl.ds(j, 1), :] = top
        istat[which + 2, pl.ds(j, 1), :] = jnp.sum(total, axis=0, keepdims=True)

    def tile(step, carry):
        k, c = step // CHUNKS, lax.rem(step, CHUNKS)
        j = c * WINDOW + k
        for n in range(CHUNKS):
            if n == CHUNKS - 1:
                @pl.when(step == CHUNKS)
                def _():
                    text_arrives(2, n)
                    send_text(2, n)
            @pl.when(step == 3 * CHUNKS + n)
            def _(n=n):
                text_arrives(3, n)
        rows = rows_of(j * CR, CR)
        s_buf[...] = lax.dot_general(txt_s[rows, :], img_s[...], NT, preferred_element_type=F32) * scale_s
        t_buf[...] = lax.dot_general(txt_t[rows, :], img_t[...], NT, preferred_element_type=F32) * scale_t
        tile_stats(j, s_buf, e_img_s, e_txt_s, 0)
        tile_stats(j, t_buf, e_img_t, e_txt_t, 1)
        return carry

    lax.fori_loop(0, TILES, tile, 0)

    tst[...] = jnp.transpose(tcol[...])[0:8, :]

    def text_stat_copy(i, c):
        shift = SHIFTS[i]
        low, high = max(0, shift), min(WINDOW, WINDOW + shift)
        size = (high - low) * CR
        here, there = (c * WINDOW + low) * CR, (c * WINDOW + low - shift) * CR
        return remote(
            tst.at[:, pl.ds(here, size)], rts.at[i, :, pl.ds(there, size)],
            ts_send.at[i, c], ts_recv.at[i, c], at(shift, c),
        )

    text_stat_copies = [text_stat_copy(i, c) for i in range(6) for c in range(CHUNKS)]
    for copy in text_stat_copies:
        copy.start()

    for which in (0, 1):
        tops, totals = istat[which], istat[which + 2]
        top = jnp.max(tops, axis=0, keepdims=True)
        ist[which : which + 1, :] = top
        ist[which + 2 : which + 3, :] = jnp.sum(totals * jnp.exp(tops - top), axis=0, keepdims=True)

    def image_stat_copy(r):
        return remote(ist, rist.at[r - 1], is_send.at[r - 1], is_recv.at[r - 1], (d, mates[r]))

    for r in (1, 2, 3):
        image_stat_copy(r).start()
    for r in (1, 2, 3):
        image_stat_copy(r).wait_recv()

    def joined(parts):
        top = functools.reduce(jnp.maximum, [a[0:2] for a in parts])
        total = functools.reduce(jnp.add, [a[2:4] * jnp.exp(a[0:2] - top) for a in parts])
        return top, total

    top, total = joined([ist[0:4, :]] + [rist[r, 0:4, :] for r in range(3)])
    for which in (0, 1):
        asc[which] = jnp.exp(istat[which] - top[which : which + 1]) / total[which : which + 1]

    for copy in text_stat_copies:
        copy.wait_recv()
    for j in range(TILES):
        cols = pl.ds(j * CR, CR)
        parts = [tst[0:4, cols]]
        for i, shift in enumerate(SHIFTS):
            if 0 <= j % WINDOW + shift < WINDOW:
                parts.append(rts[i, 0:4, cols])
        top, total = joined(parts)
        tsct[0:2, cols] = jnp.exp(tst[0:2, cols] - top) / total
    tsc[...] = jnp.transpose(tsct[...])

    def weights(j):
        a_s, a_t = asc[0, pl.ds(j, 1), :], asc[1, pl.ds(j, 1), :]

        def slab(g, carry):
            rows = rows_of(j * CR + g * SLAB, SLAB)
            c_s, c_t = tsc[rows, 0:1], tsc[rows, 1:2]
            w[rows, :] = (
                e_img_s[rows, :] * a_s - e_img_t[rows, :] * a_t
                + e_txt_s[rows, :] * c_s - e_txt_t[rows, :] * c_t
            ).astype(BF16)
            return carry

        lax.fori_loop(0, CR // SLAB, slab, 0)

    def text_term(j):
        weights(j)
        return lax.dot_general(
            w[rows_of(j * CR, CR), :], img_s[...], NN, preferred_element_type=F32
        ) * scale_s

    def grad_copies(hop, c):
        rows = pl.ds(c * CR, CR)
        return [
            remote(g_send.at[hop, rows], g_recv.at[hop, rows], g_ssem.at[hop, c, 0], g_rsem.at[hop, c, 0], at(1, c)),
            remote(g_stop.at[hop, c], g_rtop.at[hop, c], g_ssem.at[hop, c, 1], g_rsem.at[hop, c, 1], at(1, c)),
        ]

    def send_grad(hop, c, value):
        g_send[hop, pl.ds(c * CR, CR), :], g_stop[hop, c] = encoded(value)
        for copy in grad_copies(hop, c):
            copy.start()

    for c in range(CHUNKS):
        send_grad(0, c, text_term(c * WINDOW + 3))

    def earlier(n, carry):
        j = lax.rem(n, CHUNKS) * WINDOW + 2 - n // CHUNKS
        p_own[rows_of(j * CR, CR), :] = text_term(j)
        return carry

    lax.fori_loop(0, 3 * CHUNKS, earlier, 0)

    def image_term(quarter):
        return lax.dot_general(
            w[:, rows_of(quarter * ROWS, ROWS)], txt_s[...], TN, preferred_element_type=F32
        ) * scale_s

    order = (sib, diag, far, p)

    def sib_copy(i):
        return remote(gi.at[i], gi_sib.at[i], gi_ssem.at[i], gi_rsem.at[i], (d, sib))

    for i in (1, 0):
        gi[i] = image_term(order[i])
        sib_copy(i).start()
    for i in (2, 3):
        gi[i] = image_term(order[i])
    sib_copy(1).wait_recv()
    far_copies = [
        remote(x_send, x_recv, gi_ssem.at[2], gi_rsem.at[2], (d, far)),
        remote(x_stop, x_rtop, gi_ssem.at[3], gi_rsem.at[3], (d, far)),
    ]
    x_send[...], x_stop[...] = encoded(gi[2] + gi_sib[1])
    for copy in far_copies:
        copy.start()

    for hop in range(3):
        for c in range(CHUNKS):
            rows = pl.ds(c * CR, CR)
            mine = p_own[pl.ds((c * WINDOW + 2 - hop) * CR, CR), :]
            for copy in grad_copies(hop, c):
                copy.wait_recv()
            value = mine + decoded(g_recv[hop, rows, :], g_rtop[hop, c])
            if hop < 2:
                send_grad(hop + 1, c, value)
            else:
                out_text[rows, :] = value
        if hop == 1:
            sib_copy(0).wait_recv()
            for copy in far_copies:
                copy.wait_recv()
            out_image[...] = gi[3] + gi_sib[0] + decoded(x_recv[...], x_rtop[...])

    for k in range(3):
        for c in range(CHUNKS):
            for copy in text_copies(k, c) + grad_copies(k, c):
                copy.wait_send()
    for copy in to_sib + pass_on + sum(to_far, []) + text_stat_copies + far_copies:
        copy.wait_send()
    for r in (1, 2, 3):
        image_stat_copy(r).wait_send()
    for i in (0, 1):
        sib_copy(i).wait_send()


def on_device(groups, student_image, student_text, teacher_image, teacher_text):
    ds, dt = student_image.shape[1], teacher_image.shape[1]
    dma = pltpu.SemaphoreType.DMA
    vmem = pltpu.VMEM
    return pl.pallas_call(
        functools.partial(kernel, groups, 2.0 / math.sqrt(ds), 2.0 / math.sqrt(dt)),
        out_shape=(
            jax.ShapeDtypeStruct((ROWS, ds), F32),
            jax.ShapeDtypeStruct((ROWS, ds), F32),
        ),
        in_specs=[pl.BlockSpec(memory_space=pl.ANY)] * 4,
        out_specs=(pl.BlockSpec(memory_space=pltpu.VMEM),) * 2,
        scratch_shapes=[
            vmem((BLOCK, ds), BF16), vmem((BLOCK, dt), BF16),
            vmem((BLOCK, ds), BF16), vmem((BLOCK, dt), BF16),
            vmem((CR, BLOCK), F32), vmem((CR, BLOCK), F32),
            vmem((BLOCK, BLOCK), F32), vmem((BLOCK, BLOCK), F32),
            vmem((BLOCK, BLOCK), F32), vmem((BLOCK, BLOCK), F32),
            vmem((BLOCK, BLOCK), BF16),
            vmem((4, TILES, BLOCK), F32), vmem((8, BLOCK), F32), vmem((3, 8, BLOCK), F32),
            vmem((BLOCK, 128), F32), vmem((8, BLOCK), F32), vmem((6, 8, BLOCK), F32),
            vmem((128, BLOCK), F32), vmem((BLOCK, 128), F32), vmem((2, TILES, BLOCK), F32),
            vmem((3, ROWS, ds), BF16), vmem((3, ROWS, ds), BF16),
            vmem((3, CHUNKS, 8, 128), F32), vmem((3, CHUNKS, 8, 128), F32),
            vmem((BLOCK, ds), F32), vmem((4, ROWS, ds), F32), vmem((2, ROWS, ds), F32),
            vmem((ROWS, ds), BF16), vmem((ROWS, ds), BF16), vmem((8, 128), F32), vmem((8, 128), F32),
            dma((2 + 2 * CHUNKS,)), dma((2, 3, CHUNKS)), dma((2, 3, CHUNKS)),
            dma((2, 2 + PIECES)), dma((2, 2 + PIECES)),
            dma((6, CHUNKS)), dma((6, CHUNKS)), dma((3,)), dma((3,)),
            dma((3, CHUNKS, 2)), dma((3, CHUNKS, 2)), dma((4,)), dma((4,)),
        ],
        compiler_params=pltpu.CompilerParams(
            collective_id=0, has_side_effects=True, vmem_limit_bytes=56 * 2**20
        ),
    )(student_image, student_text, teacher_image, teacher_text)


def solution(mesh):
    spec = P(("dp", "pair"), None)
    return jax.shard_map(
        functools.partial(on_device, mesh.shape["dp"]),
        mesh=mesh,
        in_specs=(spec,) * 4,
        out_specs=(spec, spec),
        check_vma=False,
    )
```

```python
import functools
import math

import jax
import jax.numpy as jnp
from jax import lax
from jax.experimental import pallas as pl
from jax.experimental.pallas import tpu as pltpu
from jax.sharding import PartitionSpec as P

MESH = pl.DeviceIdType.MESH
F32 = jnp.float32
BF16 = jnp.bfloat16

WINDOW = 4
PAIR = 4
ROWS = 256
BLOCK = ROWS * PAIR
CHUNKS = 2
CR = ROWS // CHUNKS
TILES = WINDOW * CHUNKS
SLAB = 32
SHIFTS = (-3, -2, -1, 1, 2, 3)
LINE = 8
PIECES = 4
NT = (((1,), (1,)), ((), ()))
NN = (((1,), (0,)), ((), ()))
TN = (((0,), (0,)), ((), ()))


SPAN, LOW = 240.0 * math.log(2.0), 120.0 * math.log(2.0)


def rows_of(start, size):
    return pl.ds(pl.multiple_of(start, size), size)


def encoded(x):
    rows, width = x.shape
    parts = jnp.abs(x).reshape(rows // 8, 8, width)
    top = jnp.max(parts, axis=0)
    top = functools.reduce(jnp.maximum, [top[:, i : i + 128] for i in range(0, width, 128)])
    top = jnp.maximum(top, 1e-36)
    ratio = jnp.concatenate([SPAN / top] * (width // 128), axis=1)
    size = jnp.exp(parts * ratio[None] - LOW).reshape(rows, width)
    return jnp.where(x < 0, -size, size).astype(BF16), top


def decoded(code, top):
    rows, width = code.shape
    y = code.astype(F32)
    size = (jnp.log(jnp.abs(y)) + LOW).reshape(rows // 8, 8, width)
    scale = jnp.concatenate([top * (1.0 / SPAN)] * (width // 128), axis=1)
    x = (size * scale[None]).reshape(rows, width)
    return jnp.where(y < 0, -x, x)


def kernel(
    groups, scale_s, scale_t,
    si, st, ti, tt, out_image, out_text,
    img_s, img_t, txt_s, txt_t,
    s_buf, t_buf, e_img_s, e_img_t, e_txt_s, e_txt_t, w,
    istat, ist, rist, tcol, tst, rts, tsct, tsc, asc,
    g_send, g_recv, g_stop, g_rtop, p_own, gi, gi_sib, x_send, x_recv, x_stop, x_rtop,
    local_sem, tx_send, tx_recv, im_send, im_recv,
    ts_send, ts_recv, is_send, is_recv, g_ssem, g_rsem, gi_ssem, gi_rsem,
):
    d = lax.axis_index("dp")
    p = lax.axis_index("pair")
    sib = p + 1 - 2 * lax.rem(p, 2)
    far = lax.rem(p + 2, PAIR)
    diag = 3 - p
    mates = {1: sib, 2: far, 3: diag}

    place = lax.rem(d, LINE)
    last = place == LINE - 1

    def at(shift, c):
        group = lax.rem(d + shift + groups, groups)
        turns = jnp.logical_or(place + shift < 0, place + shift >= LINE)
        changes = jnp.logical_and(turns, lax.rem(p + c, 2) == 1)
        return (group, jnp.where(changes, far, p))

    def remote(src, dst, ssem, rsem, device):
        return pltpu.make_async_remote_copy(
            src_ref=src, dst_ref=dst, send_sem=ssem, recv_sem=rsem,
            device_id=device, device_id_type=MESH,
        )

    own_rows = rows_of(p * ROWS, ROWS)
    locals_ = [
        pltpu.make_async_copy(si, img_s.at[own_rows], local_sem.at[0]),
        pltpu.make_async_copy(ti, img_t.at[own_rows], local_sem.at[1]),
    ]
    for c in range(CHUNKS):
        for i, (src, buf) in enumerate(((st, txt_s), (tt, txt_t))):
            locals_.append(pltpu.make_async_copy(
                src.at[pl.ds(c * CR, CR)], buf.at[pl.ds(c * WINDOW * CR, CR)], local_sem.at[2 + 2 * c + i]
            ))
    for copy in locals_:
        copy.start()

    barrier = pltpu.get_barrier_semaphore()
    for shift in SHIFTS:
        group = lax.rem(d + shift + groups, groups)
        for other in (p, far):
            pl.semaphore_signal(barrier, inc=1, device_id=(group, other), device_id_type=MESH)
    for r in (1, 2, 3):
        pl.semaphore_signal(barrier, inc=1, device_id=(d, mates[r]), device_id_type=MESH)
    for copy in locals_:
        copy.wait()
    pl.semaphore_wait(barrier, 15)

    def text_copies(k, c):
        here, there = pl.ds((c * WINDOW + k) * CR, CR), pl.ds((c * WINDOW + k + 1) * CR, CR)
        return [
            remote(buf.at[here], buf.at[there], tx_send.at[i, k, c], tx_recv.at[i, k, c], at(-1, c))
            for i, buf in enumerate((txt_s, txt_t))
        ]

    def send_text(k, c):
        for copy in text_copies(k, c):
            copy.start()

    def text_arrives(k, c):
        for copy in text_copies(k - 1, c):
            copy.wait_recv()

    def image_copies(slot, start, size, device):
        rows = rows_of(start, size)
        return [
            remote(buf.at[rows], buf.at[rows], im_send.at[i, slot], im_recv.at[i, slot], device)
            for i, buf in enumerate((img_s, img_t))
        ]

    size = ROWS // PIECES
    to_far = [image_copies(2 + i, p * ROWS + i * size, size, (d, far)) for i in range(PIECES)]
    to_sib = image_copies(0, p * ROWS, ROWS, (d, sib))
    pass_on = image_copies(1, far * ROWS, ROWS, (d, sib))

    def send_far(i):
        for copy in to_far[i]:
            copy.start()

    for copy in to_sib:
        copy.start()
    send_text(0, 0)
    send_far(0)
    for c in range(1, CHUNKS):
        send_text(0, c)

    for i in range(1, PIECES):
        send_far(i)

    early = [(1, c) for c in range(CHUNKS)] + [(2, c) for c in range(CHUNKS - 1)]
    for i, (k, c) in enumerate(early):
        text_arrives(k, c)
        send_text(k, c)
    for piece in to_far:
        for copy in piece:
            copy.wait_recv()
    for copy in pass_on:
        copy.start()
    for copy in to_sib + pass_on:
        copy.wait_recv()

    tcol[...] = jnp.zeros_like(tcol)
    ist[...] = jnp.zeros_like(ist)
    tsct[...] = jnp.zeros_like(tsct)

    def tile_stats(j, buf, e_img, e_txt, which):
        base = j * CR

        def by_text(g, top):
            x = buf[rows_of(g * SLAB, SLAB), :]
            m = jnp.max(x, axis=1, keepdims=True)
            e = jnp.exp(x - m)
            rows = rows_of(base + g * SLAB, SLAB)
            e_txt[rows, :] = e
            tcol[rows, which : which + 1] = m
            tcol[rows, which + 2 : which + 3] = jnp.sum(e, axis=1, keepdims=True)
            return jnp.maximum(top, jnp.max(x.reshape(SLAB // 8, 8, BLOCK), axis=0))

        top = lax.fori_loop(0, CR // SLAB, by_text, jnp.full((8, BLOCK), -jnp.inf, F32))
        top = jnp.max(top, axis=0, keepdims=True)

        def by_image(g, total):
            e = jnp.exp(buf[rows_of(g * SLAB, SLAB), :] - top)
            e_img[rows_of(base + g * SLAB, SLAB), :] = e
            return total + jnp.sum(e.reshape(SLAB // 8, 8, BLOCK), axis=0)

        total = lax.fori_loop(0, CR // SLAB, by_image, jnp.zeros((8, BLOCK), F32))
        istat[which, pl.ds(j, 1), :] = top
        istat[which + 2, pl.ds(j, 1), :] = jnp.sum(total, axis=0, keepdims=True)

    def tile(step, carry):
        k, c = step // CHUNKS, lax.rem(step, CHUNKS)
        j = c * WINDOW + k
        for n in range(CHUNKS):
            if n == CHUNKS - 1:
                @pl.when(step == CHUNKS)
                def _():
                    text_arrives(2, n)
                    send_text(2, n)
            @pl.when(step == 3 * CHUNKS + n)
            def _(n=n):
                text_arrives(3, n)
        rows = rows_of(j * CR, CR)
        s_buf[...] = lax.dot_general(txt_s[rows, :], img_s[...], NT, preferred_element_type=F32) * scale_s
        t_buf[...] = lax.dot_general(txt_t[rows, :], img_t[...], NT, preferred_element_type=F32) * scale_t
        tile_stats(j, s_buf, e_img_s, e_txt_s, 0)
        tile_stats(j, t_buf, e_img_t, e_txt_t, 1)
        return carry

    lax.fori_loop(0, TILES, tile, 0)

    tst[...] = jnp.transpose(tcol[...])[0:8, :]

    def text_stat_copy(i, c):
        shift = SHIFTS[i]
        low, high = max(0, shift), min(WINDOW, WINDOW + shift)
        size = (high - low) * CR
        here, there = (c * WINDOW + low) * CR, (c * WINDOW + low - shift) * CR
        return remote(
            tst.at[:, pl.ds(here, size)], rts.at[i, :, pl.ds(there, size)],
            ts_send.at[i, c], ts_recv.at[i, c], at(shift, c),
        )

    text_stat_copies = [text_stat_copy(i, c) for i in range(6) for c in range(CHUNKS)]
    for copy in text_stat_copies:
        copy.start()

    for which in (0, 1):
        tops, totals = istat[which], istat[which + 2]
        top = jnp.max(tops, axis=0, keepdims=True)
        ist[which : which + 1, :] = top
        ist[which + 2 : which + 3, :] = jnp.sum(totals * jnp.exp(tops - top), axis=0, keepdims=True)

    def image_stat_copy(r):
        return remote(ist, rist.at[r - 1], is_send.at[r - 1], is_recv.at[r - 1], (d, mates[r]))

    for r in (1, 2, 3):
        image_stat_copy(r).start()
    for r in (1, 2, 3):
        image_stat_copy(r).wait_recv()

    def joined(parts):
        top = functools.reduce(jnp.maximum, [a[0:2] for a in parts])
        total = functools.reduce(jnp.add, [a[2:4] * jnp.exp(a[0:2] - top) for a in parts])
        return top, total

    top, total = joined([ist[0:4, :]] + [rist[r, 0:4, :] for r in range(3)])
    for which in (0, 1):
        asc[which] = jnp.exp(istat[which] - top[which : which + 1]) / total[which : which + 1]

    for copy in text_stat_copies:
        copy.wait_recv()
    for j in range(TILES):
        cols = pl.ds(j * CR, CR)
        parts = [tst[0:4, cols]]
        for i, shift in enumerate(SHIFTS):
            if 0 <= j % WINDOW + shift < WINDOW:
                parts.append(rts[i, 0:4, cols])
        top, total = joined(parts)
        tsct[0:2, cols] = jnp.exp(tst[0:2, cols] - top) / total
    tsc[...] = jnp.transpose(tsct[...])

    def weights(j):
        a_s, a_t = asc[0, pl.ds(j, 1), :], asc[1, pl.ds(j, 1), :]

        def slab(g, carry):
            rows = rows_of(j * CR + g * SLAB, SLAB)
            c_s, c_t = tsc[rows, 0:1], tsc[rows, 1:2]
            w[rows, :] = (
                e_img_s[rows, :] * a_s - e_img_t[rows, :] * a_t
                + e_txt_s[rows, :] * c_s - e_txt_t[rows, :] * c_t
            ).astype(BF16)
            return carry

        lax.fori_loop(0, CR // SLAB, slab, 0)

    def text_term(j):
        weights(j)
        return lax.dot_general(
            w[rows_of(j * CR, CR), :], img_s[...], NN, preferred_element_type=F32
        ) * scale_s

    def grad_copies(hop, c):
        rows = pl.ds(c * CR, CR)
        return [
            remote(g_send.at[hop, rows], g_recv.at[hop, rows], g_ssem.at[hop, c, 0], g_rsem.at[hop, c, 0], at(1, c)),
            remote(g_stop.at[hop, c], g_rtop.at[hop, c], g_ssem.at[hop, c, 1], g_rsem.at[hop, c, 1], at(1, c)),
        ]

    def send_grad(hop, c, value):
        g_send[hop, pl.ds(c * CR, CR), :], g_stop[hop, c] = encoded(value)
        for copy in grad_copies(hop, c):
            copy.start()

    for c in range(CHUNKS):
        send_grad(0, c, text_term(c * WINDOW + 3))

    def earlier(n, carry):
        j = lax.rem(n, CHUNKS) * WINDOW + 2 - n // CHUNKS
        p_own[rows_of(j * CR, CR), :] = text_term(j)
        return carry

    lax.fori_loop(0, 3 * CHUNKS, earlier, 0)

    def image_term(quarter):
        return lax.dot_general(
            w[:, rows_of(quarter * ROWS, ROWS)], txt_s[...], TN, preferred_element_type=F32
        ) * scale_s

    order = (sib, diag, far, p)

    def sib_copy(i):
        return remote(gi.at[i], gi_sib.at[i], gi_ssem.at[i], gi_rsem.at[i], (d, sib))

    for i in (1, 0):
        gi[i] = image_term(order[i])
        sib_copy(i).start()
    for i in (2, 3):
        gi[i] = image_term(order[i])
    sib_copy(1).wait_recv()
    far_copies = [
        remote(x_send, x_recv, gi_ssem.at[2], gi_rsem.at[2], (d, far)),
        remote(x_stop, x_rtop, gi_ssem.at[3], gi_rsem.at[3], (d, far)),
    ]
    x_send[...], x_stop[...] = encoded(gi[2] + gi_sib[1])
    for copy in far_copies:
        copy.start()

    for hop in range(3):
        for c in range(CHUNKS):
            rows = pl.ds(c * CR, CR)
            mine = p_own[pl.ds((c * WINDOW + 2 - hop) * CR, CR), :]
            for copy in grad_copies(hop, c):
                copy.wait_recv()
            value = mine + decoded(g_recv[hop, rows, :], g_rtop[hop, c])
            if hop < 2:
                send_grad(hop + 1, c, value)
            else:
                out_text[rows, :] = value
        if hop == 1:
            sib_copy(0).wait_recv()
            for copy in far_copies:
                copy.wait_recv()
            out_image[...] = gi[3] + gi_sib[0] + decoded(x_recv[...], x_rtop[...])

    for k in range(3):
        for c in range(CHUNKS):
            for copy in text_copies(k, c) + grad_copies(k, c):
                copy.wait_send()
    for copy in to_sib + pass_on + sum(to_far, []) + text_stat_copies + far_copies:
        copy.wait_send()
    for r in (1, 2, 3):
        image_stat_copy(r).wait_send()
    for i in (0, 1):
        sib_copy(i).wait_send()


def on_device(groups, student_image, student_text, teacher_image, teacher_text):
    ds, dt = student_image.shape[1], teacher_image.shape[1]
    dma = pltpu.SemaphoreType.DMA
    vmem = pltpu.VMEM
    return pl.pallas_call(
        functools.partial(kernel, groups, 2.0 / math.sqrt(ds), 2.0 / math.sqrt(dt)),
        out_shape=(
            jax.ShapeDtypeStruct((ROWS, ds), F32),
            jax.ShapeDtypeStruct((ROWS, ds), F32),
        ),
        in_specs=[pl.BlockSpec(memory_space=pl.ANY)] * 4,
        out_specs=(pl.BlockSpec(memory_space=pltpu.VMEM),) * 2,
        scratch_shapes=[
            vmem((BLOCK, ds), BF16), vmem((BLOCK, dt), BF16),
            vmem((BLOCK, ds), BF16), vmem((BLOCK, dt), BF16),
            vmem((CR, BLOCK), F32), vmem((CR, BLOCK), F32),
            vmem((BLOCK, BLOCK), F32), vmem((BLOCK, BLOCK), F32),
            vmem((BLOCK, BLOCK), F32), vmem((BLOCK, BLOCK), F32),
            vmem((BLOCK, BLOCK), BF16),
            vmem((4, TILES, BLOCK), F32), vmem((8, BLOCK), F32), vmem((3, 8, BLOCK), F32),
            vmem((BLOCK, 128), F32), vmem((8, BLOCK), F32), vmem((6, 8, BLOCK), F32),
            vmem((128, BLOCK), F32), vmem((BLOCK, 128), F32), vmem((2, TILES, BLOCK), F32),
            vmem((3, ROWS, ds), BF16), vmem((3, ROWS, ds), BF16),
            vmem((3, CHUNKS, 8, 128), F32), vmem((3, CHUNKS, 8, 128), F32),
            vmem((BLOCK, ds), F32), vmem((4, ROWS, ds), F32), vmem((2, ROWS, ds), F32),
            vmem((ROWS, ds), BF16), vmem((ROWS, ds), BF16), vmem((8, 128), F32), vmem((8, 128), F32),
            dma((2 + 2 * CHUNKS,)), dma((2, 3, CHUNKS)), dma((2, 3, CHUNKS)),
            dma((2, 2 + PIECES)), dma((2, 2 + PIECES)),
            dma((6, CHUNKS)), dma((6, CHUNKS)), dma((3,)), dma((3,)),
            dma((3, CHUNKS, 2)), dma((3, CHUNKS, 2)), dma((4,)), dma((4,)),
        ],
        compiler_params=pltpu.CompilerParams(
            collective_id=0, has_side_effects=True, vmem_limit_bytes=56 * 2**20
        ),
    )(student_image, student_text, teacher_image, teacher_text)


def solution(mesh):
    spec = P(("dp", "pair"), None)
    return jax.shard_map(
        functools.partial(on_device, mesh.shape["dp"]),
        mesh=mesh,
        in_specs=(spec,) * 4,
        out_specs=(spec, spec),
        check_vma=False,
    )
```

```python
import functools
import math

import jax
import jax.numpy as jnp
from jax import lax
from jax.experimental import pallas as pl
from jax.experimental.pallas import tpu as pltpu
from jax.sharding import PartitionSpec as P

MESH = pl.DeviceIdType.MESH
F32 = jnp.float32
BF16 = jnp.bfloat16

WINDOW = 4
PAIR = 4
ROWS = 256
BLOCK = ROWS * PAIR
CHUNKS = 2
CR = ROWS // CHUNKS
TILES = WINDOW * CHUNKS
SLAB = 128
SHORT = 96
SHIFTS = (-3, -2, -1, 1, 2, 3)
LINE = 8
PIECES = 4
NT = (((1,), (1,)), ((), ()))
NN = (((1,), (0,)), ((), ()))
TN = (((0,), (0,)), ((), ()))


SPAN, LOW = 240.0 * math.log(2.0), 120.0 * math.log(2.0)


def rows_of(start, size):
    return pl.ds(pl.multiple_of(start, size), size)


def encoded(x):
    rows, width = x.shape
    parts = jnp.abs(x).reshape(rows // 8, 8, width)
    top = jnp.max(parts, axis=0)
    top = functools.reduce(jnp.maximum, [top[:, i : i + 128] for i in range(0, width, 128)])
    top = jnp.maximum(top, 1e-36)
    ratio = jnp.concatenate([SPAN / top] * (width // 128), axis=1)
    size = jnp.exp(parts * ratio[None] - LOW).reshape(rows, width)
    return jnp.where(x < 0, -size, size).astype(BF16), top


def decoded(code, top):
    rows, width = code.shape
    y = code.astype(F32)
    size = (jnp.log(jnp.abs(y)) + LOW).reshape(rows // 8, 8, width)
    scale = jnp.concatenate([top * (1.0 / SPAN)] * (width // 128), axis=1)
    x = (size * scale[None]).reshape(rows, width)
    return jnp.where(y < 0, -x, x)


def kernel(
    groups, scale_s, scale_t,
    si, st, ti, tt, out_image, out_text,
    img_s, img_t, txt_s, txt_t,
    s_buf, t_buf, e_img_s, e_img_t, e_txt_s, e_txt_t, w,
    istat, ist, rist, tcol, tst, rts, tsct, tsc, asc,
    relay_s, relay_t, g_send, g_recv, g_stop, g_rtop, p_own, gi, gi_sib, x_send, x_recv, x_stop, x_rtop,
    local_sem, tx_send, tx_recv, lw_send, lw_recv, im_send, im_recv,
    ts_send, ts_recv, is_send, is_recv, g_ssem, g_rsem, gi_ssem, gi_rsem,
):
    d = lax.axis_index("dp")
    p = lax.axis_index("pair")
    sib = p + 1 - 2 * lax.rem(p, 2)
    far = lax.rem(p + 2, PAIR)
    diag = 3 - p
    mates = {1: sib, 2: far, 3: diag}

    place = lax.rem(d, LINE)
    last = place == LINE - 1

    def at(shift, c):
        group = lax.rem(d + shift + groups, groups)
        turns = jnp.logical_or(place + shift < 0, place + shift >= LINE)
        changes = jnp.logical_and(turns, lax.rem(p + c, 2) == 1)
        return (group, jnp.where(changes, far, p))

    def round_line(shift):
        return d - place + lax.rem(place + shift, LINE)

    def remote(src, dst, ssem, rsem, device):
        return pltpu.make_async_remote_copy(
            src_ref=src, dst_ref=dst, send_sem=ssem, recv_sem=rsem,
            device_id=device, device_id_type=MESH,
        )

    own_rows = rows_of(p * ROWS, ROWS)
    locals_ = [
        pltpu.make_async_copy(si, img_s.at[own_rows], local_sem.at[0]),
        pltpu.make_async_copy(ti, img_t.at[own_rows], local_sem.at[1]),
    ]
    for c in range(CHUNKS):
        for i, (src, buf) in enumerate(((st, txt_s), (tt, txt_t))):
            locals_.append(pltpu.make_async_copy(
                src.at[pl.ds(c * CR, CR)], buf.at[pl.ds(c * WINDOW * CR, CR)], local_sem.at[2 + 2 * c + i]
            ))
    for copy in locals_:
        copy.start()

    barrier = pltpu.get_barrier_semaphore()
    for shift in SHIFTS:
        group = lax.rem(d + shift + groups, groups)
        for other in (p, far):
            pl.semaphore_signal(barrier, inc=1, device_id=(group, other), device_id_type=MESH)
    for shift in (-6, 6):
        group = lax.rem(d + shift + groups, groups)
        for other in (p, far):
            pl.semaphore_signal(barrier, inc=1, device_id=(group, other), device_id_type=MESH)
    for shift in (3, LINE - 3):
        pl.semaphore_signal(barrier, inc=1, device_id=(round_line(shift), p), device_id_type=MESH)
    for r in (1, 2, 3):
        pl.semaphore_signal(barrier, inc=1, device_id=(d, mates[r]), device_id_type=MESH)
    for copy in locals_:
        copy.wait()
    pl.semaphore_wait(barrier, 21)

    texts = ((txt_s, relay_s), (txt_t, relay_t))

    def text_copies(k, c):
        rows = SHORT if c else CR
        here, there = pl.ds((c * WINDOW + k) * CR, rows), pl.ds((c * WINDOW + k + 1) * CR, rows)
        return [
            remote(buf.at[here], buf.at[there], tx_send.at[i, k, c], tx_recv.at[i, k, c], at(-1, c))
            for i, (buf, _) in enumerate(texts)
        ]

    def long_copies(stage):
        def rows(k):
            return pl.ds((WINDOW + k) * CR + SHORT, CR - SHORT)

        if stage == 0:
            device = (round_line(3), p)
        elif stage == 1:
            group = lax.rem(d + jnp.where(place < 3, 2, -6) + groups, groups)
            turns = jnp.logical_and(place >= 3, place < 6)
            device = (group, jnp.where(jnp.logical_and(turns, lax.rem(p + 1, 2) == 1), far, p))
        else:
            device = at(1, 1)
        copies = []
        for i, (buf, relay) in enumerate(texts):
            src = (buf.at[rows(0)], relay, buf.at[rows(3)], buf.at[rows(2)])[stage]
            dst = (relay, buf.at[rows(3)], buf.at[rows(2)], buf.at[rows(1)])[stage]
            copies.append(remote(src, dst, lw_send.at[i, stage], lw_recv.at[i, stage], device))
        return copies

    def start(copies):
        for copy in copies:
            copy.start()

    def arrive(copies):
        for copy in copies:
            copy.wait_recv()

    def image_copies(slot, quarter, device, piece=0, pieces=1):
        rows = rows_of(quarter * ROWS + piece * (ROWS // pieces), ROWS // pieces)
        return [
            remote(buf.at[rows], buf.at[rows], im_send.at[i, slot], im_recv.at[i, slot], device)
            for i, buf in enumerate((img_s, img_t))
        ]

    far_pieces = [image_copies(2 + i, p, (d, far), i, PIECES) for i in range(PIECES)]
    to_far = sum(far_pieces, [])
    to_sib = image_copies(0, p, (d, sib))
    pass_on = image_copies(1, far, (d, sib))
    start(to_sib)
    start(text_copies(0, 0))
    start(far_pieces[0])
    start(long_copies(0))
    start(text_copies(0, 1))
    start(sum(far_pieces[1:], []))
    for c in range(CHUNKS):
        arrive(text_copies(0, c))
        start(text_copies(1, c))
    arrive(long_copies(0))
    start(long_copies(1))

    def more(n):
        if n < 2:
            arrive(text_copies(1, n))
            start(text_copies(2, n))
        else:
            arrive(long_copies(1))
            start(long_copies(2))

    for n in range(3):
        more(n)

    arrive(to_far)
    start(pass_on)
    arrive(to_sib + pass_on)

    tcol[...] = jnp.zeros_like(tcol)
    ist[...] = jnp.zeros_like(ist)
    tsct[...] = jnp.zeros_like(tsct)

    def tile_stats(j, count, buf, e_img, e_txt, which):
        base = j * CR

        def by_text(g, top):
            x = buf[rows_of(g * SLAB, SLAB), :]
            m = jnp.max(x, axis=1, keepdims=True)
            e = jnp.exp(x - m)
            rows = rows_of(base + g * SLAB, SLAB)
            e_txt[rows, :] = e
            tcol[rows, which : which + 1] = m
            tcol[rows, which + 2 : which + 3] = jnp.sum(e, axis=1, keepdims=True)
            return jnp.maximum(top, jnp.max(x.reshape(SLAB // 8, 8, BLOCK), axis=0))

        top = lax.fori_loop(0, count * CR // SLAB, by_text, jnp.full((8, BLOCK), -jnp.inf, F32))
        top = jnp.max(top, axis=0, keepdims=True)

        def by_image(g, total):
            e = jnp.exp(buf[rows_of(g * SLAB, SLAB), :] - top)
            e_img[rows_of(base + g * SLAB, SLAB), :] = e
            return total + jnp.sum(e.reshape(SLAB // 8, 8, BLOCK), axis=0)

        total = lax.fori_loop(0, count * CR // SLAB, by_image, jnp.zeros((8, BLOCK), F32))
        total = jnp.sum(total, axis=0, keepdims=True)
        for n in range(count):
            istat[which, j + n : j + n + 1, :] = top
            istat[which + 2, j + n : j + n + 1, :] = total if n == 0 else jnp.zeros_like(total)

    def text_stats(c):
        cols = pl.ds(c * WINDOW * CR, WINDOW * CR)
        tst[:, cols] = jnp.transpose(tcol[cols, :])[0:8, :]

    def text_stat_copies(c):
        copies = []
        for i, shift in enumerate(SHIFTS):
            low, high = max(0, shift), min(WINDOW, WINDOW + shift)
            size = (high - low) * CR
            here, there = (c * WINDOW + low) * CR, (c * WINDOW + low - shift) * CR
            copies.append(remote(
                tst.at[:, pl.ds(here, size)], rts.at[i, :, pl.ds(there, size)],
                ts_send.at[i, c], ts_recv.at[i, c], at(shift, c),
            ))
        return copies

    def tiles(j, count):
        rows = pl.ds(j * CR, count * CR)
        here = pl.ds(0, count * CR)
        s_buf[here, :] = lax.dot_general(txt_s[rows, :], img_s[...], NT, preferred_element_type=F32) * scale_s
        t_buf[here, :] = lax.dot_general(txt_t[rows, :], img_t[...], NT, preferred_element_type=F32) * scale_t
        tile_stats(j, count, s_buf, e_img_s, e_txt_s, 0)
        tile_stats(j, count, t_buf, e_img_t, e_txt_t, 1)

    tiles(0, 2)
    tiles(WINDOW, 1)
    tiles(2, 1)
    arrive(long_copies(2))
    start(long_copies(3))
    tiles(WINDOW + 2, 1)
    arrive(long_copies(3))
    tiles(WINDOW + 1, 1)
    arrive(text_copies(2, 0))
    tiles(3, 1)
    text_stats(0)
    start(text_stat_copies(0))
    arrive(text_copies(2, 1))
    tiles(WINDOW + 3, 1)

    for which in (0, 1):
        tops, totals = istat[which], istat[which + 2]
        top = jnp.max(tops, axis=0, keepdims=True)
        ist[which : which + 1, :] = top
        ist[which + 2 : which + 3, :] = jnp.sum(totals * jnp.exp(tops - top), axis=0, keepdims=True)

    def image_stat_copy(r):
        return remote(ist, rist.at[r - 1], is_send.at[r - 1], is_recv.at[r - 1], (d, mates[r]))

    image_stat_copies = [image_stat_copy(r) for r in (1, 2, 3)]
    start(image_stat_copies)
    text_stats(1)
    start(text_stat_copies(1))

    def joined(parts):
        top = functools.reduce(jnp.maximum, [a[0:2] for a in parts])
        total = functools.reduce(jnp.add, [a[2:4] * jnp.exp(a[0:2] - top) for a in parts])
        return top, total

    def text_scales(c):
        arrive(text_stat_copies(c))
        for k in range(WINDOW):
            cols = pl.ds((c * WINDOW + k) * CR, CR)
            parts = [tst[0:4, cols]]
            for i, shift in enumerate(SHIFTS):
                if 0 <= k + shift < WINDOW:
                    parts.append(rts[i, 0:4, cols])
            top, total = joined(parts)
            tsct[0:2, cols] = jnp.exp(tst[0:2, cols] - top) / total
        cols = pl.ds(c * WINDOW * CR, WINDOW * CR)
        tsc[cols, :] = jnp.transpose(tsct[:, cols])

    text_scales(0)
    arrive(image_stat_copies)
    top, total = joined([ist[0:4, :]] + [rist[r, 0:4, :] for r in range(3)])
    for which in (0, 1):
        asc[which] = jnp.exp(istat[which] - top[which : which + 1]) / total[which : which + 1]

    def weights(j):
        a_s, a_t = asc[0, pl.ds(j, 1), :], asc[1, pl.ds(j, 1), :]

        def slab(g, carry):
            rows = rows_of(j * CR + g * SLAB, SLAB)
            c_s, c_t = tsc[rows, 0:1], tsc[rows, 1:2]
            w[rows, :] = (
                e_img_s[rows, :] * a_s - e_img_t[rows, :] * a_t
                + e_txt_s[rows, :] * c_s - e_txt_t[rows, :] * c_t
            ).astype(BF16)
            return carry

        lax.fori_loop(0, CR // SLAB, slab, 0)

    def text_term(j):
        return lax.dot_general(
            w[rows_of(j * CR, CR), :], img_s[...], NN, preferred_element_type=F32
        ) * scale_s

    def grad_copies(hop, c):
        rows = pl.ds(c * CR, CR)
        return [
            remote(g_send.at[hop, rows], g_recv.at[hop, rows], g_ssem.at[hop, c, 0], g_rsem.at[hop, c, 0], at(1, c)),
            remote(g_stop.at[hop, c], g_rtop.at[hop, c], g_ssem.at[hop, c, 1], g_rsem.at[hop, c, 1], at(1, c)),
        ]

    def send_grad(hop, c, value):
        g_send[hop, pl.ds(c * CR, CR), :], g_stop[hop, c] = encoded(value)
        start(grad_copies(hop, c))

    def pass_grad(hop, c):
        rows = pl.ds(c * CR, CR)
        mine = p_own[pl.ds((c * WINDOW + 2 - hop) * CR, CR), :]
        arrive(grad_copies(hop, c))
        value = mine + decoded(g_recv[hop, rows, :], g_rtop[hop, c])
        if hop < 2:
            send_grad(hop + 1, c, value)
        else:
            out_text[rows, :] = value

    def own_terms(k):
        def one(c, carry):
            j = c * WINDOW + k
            p_own[rows_of(j * CR, CR), :] = text_term(j)
            return carry

        lax.fori_loop(0, CHUNKS, one, 0)

    def image_term(quarter):
        return lax.dot_general(
            w[:, rows_of(quarter * ROWS, ROWS)], txt_s[...], TN, preferred_element_type=F32
        ) * scale_s

    order = (sib, diag, far, p)
    sib_copies = [remote(gi.at[i], gi_sib.at[i], gi_ssem.at[i], gi_rsem.at[i], (d, sib)) for i in (0, 1)]
    far_copies = [
        remote(x_send, x_recv, gi_ssem.at[2], gi_rsem.at[2], (d, far)),
        remote(x_stop, x_rtop, gi_ssem.at[3], gi_rsem.at[3], (d, far)),
    ]

    weights(3)
    send_grad(0, 0, text_term(3))
    text_scales(1)
    weights(WINDOW + 3)
    send_grad(0, 1, text_term(WINDOW + 3))

    def other_weights(n, carry):
        weights(lax.rem(n, CHUNKS) * WINDOW + n // CHUNKS)
        return carry

    lax.fori_loop(0, 3 * CHUNKS, other_weights, 0)
    for i in (1, 0):
        gi[i] = image_term(order[i])
        sib_copies[i].start()
    own_terms(2)
    pass_grad(0, 0)
    gi[2] = image_term(order[2])
    arrive(sib_copies[1:])
    x_send[...], x_stop[...] = encoded(gi[2] + gi_sib[1])
    start(far_copies)
    pass_grad(0, 1)
    own_terms(1)
    gi[3] = image_term(order[3])
    pass_grad(1, 0)
    own_terms(0)
    pass_grad(1, 1)
    arrive(sib_copies[:1] + far_copies)
    out_image[...] = gi[3] + gi_sib[0] + decoded(x_recv[...], x_rtop[...])
    pass_grad(2, 0)
    pass_grad(2, 1)

    for k in range(3):
        for c in range(CHUNKS):
            for copy in text_copies(k, c) + grad_copies(k, c):
                copy.wait_send()
    for copies in [long_copies(n) for n in range(4)] + [text_stat_copies(c) for c in range(CHUNKS)]:
        for copy in copies:
            copy.wait_send()
    for copy in to_far + to_sib + pass_on + image_stat_copies + sib_copies + far_copies:
        copy.wait_send()


def on_device(groups, student_image, student_text, teacher_image, teacher_text):
    ds, dt = student_image.shape[1], teacher_image.shape[1]
    dma = pltpu.SemaphoreType.DMA
    vmem = pltpu.VMEM
    return pl.pallas_call(
        functools.partial(kernel, groups, 2.0 / math.sqrt(ds), 2.0 / math.sqrt(dt)),
        out_shape=(
            jax.ShapeDtypeStruct((ROWS, ds), F32),
            jax.ShapeDtypeStruct((ROWS, ds), F32),
        ),
        in_specs=[pl.BlockSpec(memory_space=pl.ANY)] * 4,
        out_specs=(pl.BlockSpec(memory_space=pltpu.VMEM),) * 2,
        scratch_shapes=[
            vmem((BLOCK, ds), BF16), vmem((BLOCK, dt), BF16),
            vmem((BLOCK, ds), BF16), vmem((BLOCK, dt), BF16),
            vmem((2 * CR, BLOCK), F32), vmem((2 * CR, BLOCK), F32),
            vmem((BLOCK, BLOCK), F32), vmem((BLOCK, BLOCK), F32),
            vmem((BLOCK, BLOCK), F32), vmem((BLOCK, BLOCK), F32),
            vmem((BLOCK, BLOCK), BF16),
            vmem((4, TILES, BLOCK), F32), vmem((8, BLOCK), F32), vmem((3, 8, BLOCK), F32),
            vmem((BLOCK, 128), F32), vmem((8, BLOCK), F32), vmem((6, 8, BLOCK), F32),
            vmem((128, BLOCK), F32), vmem((BLOCK, 128), F32), vmem((2, TILES, BLOCK), F32),
            vmem((CR - SHORT, ds), BF16), vmem((CR - SHORT, dt), BF16),
            vmem((3, ROWS, ds), BF16), vmem((3, ROWS, ds), BF16),
            vmem((3, CHUNKS, 8, 128), F32), vmem((3, CHUNKS, 8, 128), F32),
            vmem((BLOCK, ds), F32), vmem((4, ROWS, ds), F32), vmem((2, ROWS, ds), F32),
            vmem((ROWS, ds), BF16), vmem((ROWS, ds), BF16), vmem((8, 128), F32), vmem((8, 128), F32),
            dma((2 + 2 * CHUNKS,)), dma((2, 3, CHUNKS)), dma((2, 3, CHUNKS)),
            dma((2, 4)), dma((2, 4)), dma((2, 2 + PIECES)), dma((2, 2 + PIECES)),
            dma((6, CHUNKS)), dma((6, CHUNKS)), dma((3,)), dma((3,)),
            dma((3, CHUNKS, 2)), dma((3, CHUNKS, 2)), dma((4,)), dma((4,)),
        ],
        compiler_params=pltpu.CompilerParams(
            collective_id=0, has_side_effects=True, vmem_limit_bytes=56 * 2**20
        ),
    )(student_image, student_text, teacher_image, teacher_text)


def solution(mesh):
    spec = P(("dp", "pair"), None)
    return jax.shard_map(
        functools.partial(on_device, mesh.shape["dp"]),
        mesh=mesh,
        in_specs=(spec,) * 4,
        out_specs=(spec, spec),
        check_vma=False,
    )
```

```python
import functools
import math

import jax
import jax.numpy as jnp
from jax import lax
from jax.experimental import pallas as pl
from jax.experimental.pallas import tpu as pltpu
from jax.sharding import PartitionSpec as P

MESH = pl.DeviceIdType.MESH
F32 = jnp.float32
BF16 = jnp.bfloat16

WINDOW = 4
PAIR = 4
ROWS = 256
BLOCK = ROWS * PAIR
CHUNKS = 2
CR = ROWS // CHUNKS
TILES = WINDOW * CHUNKS
SLAB = 128
SHORT = 64
SHIFTS = (-3, -2, -1, 1, 2, 3)
LINE = 8
PIECES = 4
PARTS = 2
NT = (((1,), (1,)), ((), ()))
NN = (((1,), (0,)), ((), ()))
TN = (((0,), (0,)), ((), ()))


SPAN, LOW = 240.0 * math.log(2.0), 120.0 * math.log(2.0)


def rows_of(start, size):
    return pl.ds(pl.multiple_of(start, size), size)


def encoded(x):
    rows, width = x.shape
    parts = jnp.abs(x).reshape(rows // 8, 8, width)
    top = jnp.max(parts, axis=0)
    top = functools.reduce(jnp.maximum, [top[:, i : i + 128] for i in range(0, width, 128)])
    top = jnp.maximum(top, 1e-36)
    ratio = jnp.concatenate([SPAN / top] * (width // 128), axis=1)
    size = jnp.exp(parts * ratio[None] - LOW).reshape(rows, width)
    return jnp.where(x < 0, -size, size).astype(BF16), top


def decoded(code, top):
    rows, width = code.shape
    y = code.astype(F32)
    size = (jnp.log(jnp.abs(y)) + LOW).reshape(rows // 8, 8, width)
    scale = jnp.concatenate([top * (1.0 / SPAN)] * (width // 128), axis=1)
    x = (size * scale[None]).reshape(rows, width)
    return jnp.where(y < 0, -x, x)


def kernel(
    groups, scale_s, scale_t,
    si, st, ti, tt, out_image, out_text,
    img_s, img_t, txt_s, txt_t,
    s_buf, t_buf, e_img_s, e_img_t, e_txt_s, e_txt_t, w,
    istat, ist, rist, tcol, tst, rts, tsct, tsc, asc,
    relay_s, relay_t, corner_s, corner_t, g_send, g_recv, g_stop, g_rtop, p_own, gi, gi_sib, x_send, x_recv, x_stop, x_rtop,
    local_sem, tx_send, tx_recv, cn_send, cn_recv, on_send, lw_send, lw_recv, im_send, im_recv,
    ts_send, ts_recv, is_send, is_recv, g_ssem, g_rsem, gi_ssem, gi_rsem,
):
    d = lax.axis_index("dp")
    p = lax.axis_index("pair")
    sib = p + 1 - 2 * lax.rem(p, 2)
    far = lax.rem(p + 2, PAIR)
    diag = 3 - p
    mates = {1: sib, 2: far, 3: diag}

    place = lax.rem(d, LINE)
    last = place == LINE - 1

    def at(shift, c):
        group = lax.rem(d + shift + groups, groups)
        turns = jnp.logical_or(place + shift < 0, place + shift >= LINE)
        changes = jnp.logical_and(turns, lax.rem(p + c, 2) == 1)
        return (group, jnp.where(changes, far, p))

    def round_line(shift):
        return d - place + lax.rem(place + shift, LINE)

    def remote(src, dst, ssem, rsem, device):
        return pltpu.make_async_remote_copy(
            src_ref=src, dst_ref=dst, send_sem=ssem, recv_sem=rsem,
            device_id=device, device_id_type=MESH,
        )

    own_rows = rows_of(p * ROWS, ROWS)
    locals_ = [
        pltpu.make_async_copy(si, img_s.at[own_rows], local_sem.at[0]),
        pltpu.make_async_copy(ti, img_t.at[own_rows], local_sem.at[1]),
    ]
    for c in range(CHUNKS):
        for i, (src, buf) in enumerate(((st, txt_s), (tt, txt_t))):
            locals_.append(pltpu.make_async_copy(
                src.at[pl.ds(c * CR, CR)], buf.at[pl.ds(c * WINDOW * CR, CR)], local_sem.at[2 + 2 * c + i]
            ))
    for copy in locals_:
        copy.start()

    barrier = pltpu.get_barrier_semaphore()
    for shift in SHIFTS:
        group = lax.rem(d + shift + groups, groups)
        for other in (p, far):
            pl.semaphore_signal(barrier, inc=1, device_id=(group, other), device_id_type=MESH)
    for shift in (-8, -6, 6, 8):
        group = lax.rem(d + shift + groups, groups)
        for other in (p, far):
            pl.semaphore_signal(barrier, inc=1, device_id=(group, other), device_id_type=MESH)
    for shift in (-7, 7):
        group = lax.rem(d + shift + groups, groups)
        pl.semaphore_signal(barrier, inc=1, device_id=(group, p), device_id_type=MESH)
    for shift in (3, LINE - 3):
        pl.semaphore_signal(barrier, inc=1, device_id=(round_line(shift), p), device_id_type=MESH)
    for r in (1, 2, 3):
        pl.semaphore_signal(barrier, inc=1, device_id=(d, mates[r]), device_id_type=MESH)
    for copy in locals_:
        copy.wait()
    pl.semaphore_wait(barrier, 27)

    texts = ((txt_s, relay_s), (txt_t, relay_t))

    def text_copies(k, c):
        rows = SHORT if c else CR
        here, there = pl.ds((c * WINDOW + k) * CR, rows), pl.ds((c * WINDOW + k + 1) * CR, rows)
        return [
            remote(buf.at[here], buf.at[there], tx_send.at[i, k, c], tx_recv.at[i, k, c], at(-1, c))
            for i, (buf, _) in enumerate(texts)
        ]

    corners = (corner_s, corner_t)
    first = place == 0

    def corner_copies(k):
        here = pl.ds((WINDOW + k) * CR, SHORT)
        device = (lax.rem(d - LINE + groups, groups), at(-1, 1)[1])
        return [
            remote(buf.at[here], held.at[k], cn_send.at[i, k], cn_recv.at[i, k], device)
            for i, ((buf, _), held) in enumerate(zip(texts, corners))
        ]

    def onward_copies(k):
        there = pl.ds((WINDOW + k + 1) * CR, SHORT)
        device = (lax.rem(d + LINE - 1, groups), p)
        return [
            remote(held.at[k], buf.at[there], on_send.at[i, k], tx_recv.at[i, k, 1], device)
            for i, ((buf, _), held) in enumerate(zip(texts, corners))
        ]

    def send_text(k, c):
        if c == 0:
            start(text_copies(k, 0))
            return

        @pl.when(first)
        def _():
            start(corner_copies(k))

        @pl.when(jnp.logical_not(first))
        def _():
            start(text_copies(k, 1))

    def corner_step(k):
        @pl.when(first)
        def _():
            arrive(corner_copies(k))
            start(onward_copies(k))

    def long_copies(stage, part):
        size = (CR - SHORT) // PARTS

        def rows(k):
            return pl.ds((WINDOW + k) * CR + SHORT + part * size, size)

        if stage == 0:
            device = (round_line(3), p)
        elif stage == 1:
            group = lax.rem(d + jnp.where(place < 3, 2, -6) + groups, groups)
            turns = jnp.logical_and(place >= 3, place < 6)
            device = (group, jnp.where(jnp.logical_and(turns, lax.rem(p + 1, 2) == 1), far, p))
        else:
            device = at(1, 1)
        copies = []
        for i, (buf, relay) in enumerate(texts):
            between = relay.at[pl.ds(part * size, size)]
            src = (buf.at[rows(0)], between, buf.at[rows(3)], buf.at[rows(2)])[stage]
            dst = (between, buf.at[rows(3)], buf.at[rows(2)], buf.at[rows(1)])[stage]
            copies.append(remote(src, dst, lw_send.at[i, stage, part], lw_recv.at[i, stage, part], device))
        return copies

    def start(copies):
        for copy in copies:
            copy.start()

    def arrive(copies):
        for copy in copies:
            copy.wait_recv()

    def image_copies(slot, quarter, device, piece=0, pieces=1):
        rows = rows_of(quarter * ROWS + piece * (ROWS // pieces), ROWS // pieces)
        return [
            remote(buf.at[rows], buf.at[rows], im_send.at[i, slot], im_recv.at[i, slot], device)
            for i, buf in enumerate((img_s, img_t))
        ]

    far_pieces = [image_copies(2 + i, p, (d, far), i, PIECES) for i in range(PIECES)]
    to_far = sum(far_pieces, [])
    to_sib = image_copies(0, p, (d, sib))
    pass_on = image_copies(1, far, (d, sib))
    start(to_sib)
    send_text(0, 0)
    start(long_copies(0, 0))
    start(far_pieces[0])
    for i in range(1, PARTS):
        start(long_copies(0, i))
    send_text(0, 1)
    start(sum(far_pieces[1:], []))

    def text_step(k, c):
        arrive(text_copies(k, c))
        if k < 2:
            send_text(k + 1, c)

    def long_step(stage, part):
        arrive(long_copies(stage, part))
        if stage < 3:
            start(long_copies(stage + 1, part))

    long_step(0, 0)
    corner_step(0)
    text_step(0, 0)
    text_step(0, 1)
    long_step(0, 1)
    long_step(1, 0)
    corner_step(1)

    @pl.when(last)
    def _():
        text_step(1, 0)
        long_step(1, 1)
        long_step(2, 0)

    arrive(to_far)
    start(pass_on)
    arrive(to_sib + pass_on)

    tcol[...] = jnp.zeros_like(tcol)
    ist[...] = jnp.zeros_like(ist)
    tsct[...] = jnp.zeros_like(tsct)

    def tile_stats(j, count, buf, e_img, e_txt, which):
        base = j * CR

        def by_text(g, top):
            x = buf[rows_of(g * SLAB, SLAB), :]
            m = jnp.max(x, axis=1, keepdims=True)
            e = jnp.exp(x - m)
            rows = rows_of(base + g * SLAB, SLAB)
            e_txt[rows, :] = e
            tcol[rows, which : which + 1] = m
            tcol[rows, which + 2 : which + 3] = jnp.sum(e, axis=1, keepdims=True)
            return jnp.maximum(top, jnp.max(x.reshape(SLAB // 8, 8, BLOCK), axis=0))

        top = lax.fori_loop(0, count * CR // SLAB, by_text, jnp.full((8, BLOCK), -jnp.inf, F32))
        top = jnp.max(top, axis=0, keepdims=True)

        def by_image(g, total):
            e = jnp.exp(buf[rows_of(g * SLAB, SLAB), :] - top)
            e_img[rows_of(base + g * SLAB, SLAB), :] = e
            return total + jnp.sum(e.reshape(SLAB // 8, 8, BLOCK), axis=0)

        total = lax.fori_loop(0, count * CR // SLAB, by_image, jnp.zeros((8, BLOCK), F32))
        total = jnp.sum(total, axis=0, keepdims=True)
        for n in range(count):
            istat[which, j + n : j + n + 1, :] = top
            istat[which + 2, j + n : j + n + 1, :] = total if n == 0 else jnp.zeros_like(total)

    def text_stats(c):
        cols = pl.ds(c * WINDOW * CR, WINDOW * CR)
        tst[:, cols] = jnp.transpose(tcol[cols, :])[0:8, :]

    def text_stat_copies(c):
        copies = []
        for i, shift in enumerate(SHIFTS):
            low, high = max(0, shift), min(WINDOW, WINDOW + shift)
            size = (high - low) * CR
            here, there = (c * WINDOW + low) * CR, (c * WINDOW + low - shift) * CR
            copies.append(remote(
                tst.at[:, pl.ds(here, size)], rts.at[i, :, pl.ds(there, size)],
                ts_send.at[i, c], ts_recv.at[i, c], at(shift, c),
            ))
        return copies

    def tiles(j, count):
        rows = pl.ds(j * CR, count * CR)
        here = pl.ds(0, count * CR)
        s_buf[here, :] = lax.dot_general(txt_s[rows, :], img_s[...], NT, preferred_element_type=F32) * scale_s
        t_buf[here, :] = lax.dot_general(txt_t[rows, :], img_t[...], NT, preferred_element_type=F32) * scale_t
        tile_stats(j, count, s_buf, e_img_s, e_txt_s, 0)
        tile_stats(j, count, t_buf, e_img_t, e_txt_t, 1)

    tiles(0, 2)

    @pl.when(jnp.logical_not(last))
    def _():
        text_step(1, 0)
        long_step(1, 1)
        long_step(2, 0)

    tiles(4, 1)
    text_step(1, 1)
    long_step(2, 1)
    tiles(2, 1)
    corner_step(2)
    tiles(6, 1)
    long_step(3, 0)
    long_step(3, 1)
    tiles(5, 1)
    text_step(2, 0)
    tiles(3, 1)
    text_stats(0)
    start(text_stat_copies(0))
    text_step(2, 1)
    tiles(7, 1)

    for which in (0, 1):
        tops, totals = istat[which], istat[which + 2]
        top = jnp.max(tops, axis=0, keepdims=True)
        ist[which : which + 1, :] = top
        ist[which + 2 : which + 3, :] = jnp.sum(totals * jnp.exp(tops - top), axis=0, keepdims=True)

    def image_stat_copy(r):
        return remote(ist, rist.at[r - 1], is_send.at[r - 1], is_recv.at[r - 1], (d, mates[r]))

    image_stat_copies = [image_stat_copy(r) for r in (1, 2, 3)]
    start(image_stat_copies)
    text_stats(1)
    start(text_stat_copies(1))

    def joined(parts):
        top = functools.reduce(jnp.maximum, [a[0:2] for a in parts])
        total = functools.reduce(jnp.add, [a[2:4] * jnp.exp(a[0:2] - top) for a in parts])
        return top, total

    def text_scales(c):
        arrive(text_stat_copies(c))
        for k in range(WINDOW):
            cols = pl.ds((c * WINDOW + k) * CR, CR)
            parts = [tst[0:4, cols]]
            for i, shift in enumerate(SHIFTS):
                if 0 <= k + shift < WINDOW:
                    parts.append(rts[i, 0:4, cols])
            top, total = joined(parts)
            tsct[0:2, cols] = jnp.exp(tst[0:2, cols] - top) / total
        cols = pl.ds(c * WINDOW * CR, WINDOW * CR)
        tsc[cols, :] = jnp.transpose(tsct[:, cols])

    text_scales(0)
    arrive(image_stat_copies)
    top, total = joined([ist[0:4, :]] + [rist[r, 0:4, :] for r in range(3)])
    for which in (0, 1):
        asc[which] = jnp.exp(istat[which] - top[which : which + 1]) / total[which : which + 1]

    def weights(j):
        a_s, a_t = asc[0, pl.ds(j, 1), :], asc[1, pl.ds(j, 1), :]

        def slab(g, carry):
            rows = rows_of(j * CR + g * SLAB, SLAB)
            c_s, c_t = tsc[rows, 0:1], tsc[rows, 1:2]
            w[rows, :] = (
                e_img_s[rows, :] * a_s - e_img_t[rows, :] * a_t
                + e_txt_s[rows, :] * c_s - e_txt_t[rows, :] * c_t
            ).astype(BF16)
            return carry

        lax.fori_loop(0, CR // SLAB, slab, 0)

    def text_term(j):
        return lax.dot_general(
            w[rows_of(j * CR, CR), :], img_s[...], NN, preferred_element_type=F32
        ) * scale_s

    def grad_copies(hop, c):
        rows = pl.ds(c * CR, CR)
        return [
            remote(g_send.at[hop, rows], g_recv.at[hop, rows], g_ssem.at[hop, c, 0], g_rsem.at[hop, c, 0], at(1, c)),
            remote(g_stop.at[hop, c], g_rtop.at[hop, c], g_ssem.at[hop, c, 1], g_rsem.at[hop, c, 1], at(1, c)),
        ]

    def send_grad(hop, c, value):
        g_send[hop, pl.ds(c * CR, CR), :], g_stop[hop, c] = encoded(value)
        start(grad_copies(hop, c))

    def pass_grad(hop, c):
        rows = pl.ds(c * CR, CR)
        mine = p_own[pl.ds((c * WINDOW + 2 - hop) * CR, CR), :]
        arrive(grad_copies(hop, c))
        value = mine + decoded(g_recv[hop, rows, :], g_rtop[hop, c])
        if hop < 2:
            send_grad(hop + 1, c, value)
        else:
            out_text[rows, :] = value

    def own_terms(k):
        def one(c, carry):
            j = c * WINDOW + k
            p_own[rows_of(j * CR, CR), :] = text_term(j)
            return carry

        lax.fori_loop(0, CHUNKS, one, 0)

    def image_term(quarter):
        return lax.dot_general(
            w[:, rows_of(quarter * ROWS, ROWS)], txt_s[...], TN, preferred_element_type=F32
        ) * scale_s

    order = (sib, diag, far, p)
    sib_copies = [remote(gi.at[i], gi_sib.at[i], gi_ssem.at[i], gi_rsem.at[i], (d, sib)) for i in (0, 1)]
    far_copies = [
        remote(x_send, x_recv, gi_ssem.at[2], gi_rsem.at[2], (d, far)),
        remote(x_stop, x_rtop, gi_ssem.at[3], gi_rsem.at[3], (d, far)),
    ]

    weights(3)
    send_grad(0, 0, text_term(3))
    text_scales(1)
    weights(WINDOW + 3)
    send_grad(0, 1, text_term(WINDOW + 3))

    def other_weights(n, carry):
        weights(lax.rem(n, CHUNKS) * WINDOW + n // CHUNKS)
        return carry

    lax.fori_loop(0, 3 * CHUNKS, other_weights, 0)
    for i in (1, 0):
        gi[i] = image_term(order[i])
        sib_copies[i].start()
    own_terms(2)
    pass_grad(0, 0)
    gi[2] = image_term(order[2])
    arrive(sib_copies[1:])
    x_send[...], x_stop[...] = encoded(gi[2] + gi_sib[1])
    start(far_copies)
    pass_grad(0, 1)
    own_terms(1)
    gi[3] = image_term(order[3])
    pass_grad(1, 0)
    own_terms(0)
    pass_grad(1, 1)
    arrive(sib_copies[:1] + far_copies)
    out_image[...] = gi[3] + gi_sib[0] + decoded(x_recv[...], x_rtop[...])
    pass_grad(2, 0)
    pass_grad(2, 1)

    @pl.when(first)
    def _():
        for k in range(3):
            for copy in corner_copies(k) + onward_copies(k):
                copy.wait_send()

    @pl.when(jnp.logical_not(first))
    def _():
        for k in range(3):
            for copy in text_copies(k, 1):
                copy.wait_send()

    for k in range(3):
        for copy in text_copies(k, 0) + grad_copies(k, 0) + grad_copies(k, 1):
            copy.wait_send()
    for copies in [long_copies(n, i) for n in range(4) for i in range(PARTS)] + [text_stat_copies(c) for c in range(CHUNKS)]:
        for copy in copies:
            copy.wait_send()
    for copy in to_far + to_sib + pass_on + image_stat_copies + sib_copies + far_copies:
        copy.wait_send()


def on_device(groups, student_image, student_text, teacher_image, teacher_text):
    ds, dt = student_image.shape[1], teacher_image.shape[1]
    dma = pltpu.SemaphoreType.DMA
    vmem = pltpu.VMEM
    results = pl.pallas_call(
        functools.partial(kernel, groups, 2.0 / math.sqrt(ds), 2.0 / math.sqrt(dt)),
        out_shape=(
            vmem((ROWS, ds), F32),
            vmem((ROWS, ds), F32),
        ),
        in_specs=[pl.BlockSpec(memory_space=pl.ANY)] * 4,
        out_specs=(pl.BlockSpec(memory_space=pltpu.VMEM),) * 2,
        scratch_shapes=[
            vmem((BLOCK, ds), BF16), vmem((BLOCK, dt), BF16),
            vmem((BLOCK, ds), BF16), vmem((BLOCK, dt), BF16),
            vmem((2 * CR, BLOCK), F32), vmem((2 * CR, BLOCK), F32),
            vmem((BLOCK, BLOCK), F32), vmem((BLOCK, BLOCK), F32),
            vmem((BLOCK, BLOCK), F32), vmem((BLOCK, BLOCK), F32),
            vmem((BLOCK, BLOCK), BF16),
            vmem((4, TILES, BLOCK), F32), vmem((8, BLOCK), F32), vmem((3, 8, BLOCK), F32),
            vmem((BLOCK, 128), F32), vmem((8, BLOCK), F32), vmem((6, 8, BLOCK), F32),
            vmem((128, BLOCK), F32), vmem((BLOCK, 128), F32), vmem((2, TILES, BLOCK), F32),
            vmem((CR - SHORT, ds), BF16), vmem((CR - SHORT, dt), BF16),
            vmem((3, SHORT, ds), BF16), vmem((3, SHORT, dt), BF16),
            vmem((3, ROWS, ds), BF16), vmem((3, ROWS, ds), BF16),
            vmem((3, CHUNKS, 8, 128), F32), vmem((3, CHUNKS, 8, 128), F32),
            vmem((BLOCK, ds), F32), vmem((4, ROWS, ds), F32), vmem((2, ROWS, ds), F32),
            vmem((ROWS, ds), BF16), vmem((ROWS, ds), BF16), vmem((8, 128), F32), vmem((8, 128), F32),
            dma((2 + 2 * CHUNKS,)), dma((2, 3, CHUNKS)), dma((2, 3, CHUNKS)),
            dma((2, 3)), dma((2, 3)), dma((2, 3)),
            dma((2, 4, PARTS)), dma((2, 4, PARTS)), dma((2, 2 + PIECES)), dma((2, 2 + PIECES)),
            dma((6, CHUNKS)), dma((6, CHUNKS)), dma((3,)), dma((3,)),
            dma((3, CHUNKS, 2)), dma((3, CHUNKS, 2)), dma((4,)), dma((4,)),
        ],
        compiler_params=pltpu.CompilerParams(
            collective_id=0, has_side_effects=True, vmem_limit_bytes=56 * 2**20
        ),
    )(student_image, student_text, teacher_image, teacher_text)
    return tuple(results)


def solution(mesh):
    spec = P(("dp", "pair"), None)
    return jax.shard_map(
        functools.partial(on_device, mesh.shape["dp"]),
        mesh=mesh,
        in_specs=(spec,) * 4,
        out_specs=(spec, spec),
        check_vma=False,
    )
```
